32 devices in a mesh: dom: 4 (over z), grp: 8 (over y, x, core).
Axes of the slice: x: 2, y: 2, z: 4, core: 2. Of those that a mesh axis runs over, the one named last changes fastest.
Arguments:
- src_table: float32 [4096, 400], P(('dom', 'grp')), may hold values from -8 to 8
- src_state: float32 [4096], P(('dom', 'grp')), may hold values from 0.01 to 1
- tgt_table: float32 [32768, 400], P(('dom', 'grp')), may hold values from -8 to 8
- tgt_state: float32 [32768], P(('dom', 'grp')), may hold values from 0.01 to 1
- pair_source: int32 [2, 32768], P(None, ('dom', 'grp')), may hold values from 0 to 127
- pair_owner: int32 [2, 32768, 1], P(None, ('dom', 'grp')), may hold values from 0 to 7; in each aligned block of 1024 rows (0 to 1023, 1024 to 2047, ..., all dimensions but the last counted through in order) at most 256 rows name the same one
- pair_offset: int32 [2, 32768], P(None, ('dom', 'grp')), may hold values from 0 to 1023
- negatives: int32 [4, 1000], P('dom'), may hold values from 0 to 8191
- plan: int32 [2, 4], replicated, may hold values from 0 to 3, each once within a row
Outputs:
- src_trained: float32 [4096, 400], P(('dom', 'grp'))
- src_accum: float32 [4096], P(('dom', 'grp'))
- tgt_trained: float32 [32768, 400], P(('dom', 'grp'))
- tgt_accum: float32 [32768], P(('dom', 'grp'))
The draws below stay inside these ranges and needn't reach their ends.
Inputs may be any that keep to these rules, and one draw needn't show every extreme that they name: `pair_owner`: in every round the pairs of one device name each owner at most 256 times, and some device's pairs name some owner exactly 256 times. `plan`: each round's row names every dom index once.
All inputs are finite; a program needn't handle non-finite values.
Results may differ from the reference program's by a relative error of at most 0.011.
Values may be sent and summed in bfloat16 or wider, within the bound.
A program may use at most 128 MiB of HBM per device.

```python
import math
import jax
import jax.numpy as jnp
import numpy as np
from jax import lax

D = 400
NEG = 1000
ROUNDS = 2
SRC_DEV = 128
TGT_DEV = 1024
PAIR_DEV = 1024
CAP = 256
PAIRS = 32768
SRC_ROWS = 4096
TGT_ROWS = 32768
N_DOM = 4
N_GRP = 8


def table_values(key, row_total):
    return jnp.clip(0.4 * jax.random.normal(key, (row_total, D), jnp.float32), -2.4, 2.4)


def draw_src_table(key, part):
    return table_values(jax.random.fold_in(key, 11), SRC_ROWS)


def draw_tgt_table(key, part):
    return table_values(jax.random.fold_in(key, 23), TGT_ROWS)


def plant(result, stream_key, least, high):
    longest = result.shape.index(max(result.shape))
    spots = []
    for shift in (0, 1):
        where = [jax.random.randint(jax.random.fold_in(stream_key, axis), (), 0, length) for axis, length in enumerate(result.shape)]
        where[longest] = (where[longest] + shift) % result.shape[longest]
        spots.append(tuple(where))
    return result.at[spots[0]].set(least).at[spots[1]].set(high)


def steps_of(key, dims, pieces, least, top_value):
    loudness, own = 1.0, jax.random.fold_in(key, 6)
    for dim, shards_of in pieces:
        draws = jnp.exp(jax.random.uniform(jax.random.fold_in(own, dim), (shards_of,), jnp.float32, least / len(pieces), top_value / len(pieces)))
        loudness = loudness * jnp.repeat(draws, dims[dim] // shards_of).reshape([-1 if axis == dim else 1 for axis in range(len(dims))])
    return loudness


def deal_out(key, own, number, rows, count, top, bound, lean):
    ranking = jax.random.permutation(key, count)
    packed, usual = load_shares(count, rows * top, bound, lean, True), load_shares(count, rows * top, bound, lean, False)
    places = jnp.arange(count)

    def named(tallies, rotation):
        used = int((tallies > 0).sum())
        fixed = max(1, used // 4)
        moved = fixed + (places - fixed + rotation * (used - fixed)) % max(1, count - fixed)
        return jnp.zeros((count,), jnp.int32).at[ranking[jnp.where(places < fixed, places, moved)]].set(jnp.asarray(tallies, jnp.int32))

    tallies = jnp.where(number % 4 == 0, named(packed, number // 4), named(usual, number - number // 4 - 1))
    mixed = jax.random.permutation(jax.random.fold_in(own, 3), count)
    donor, taker = mixed[0:count // 2 * 2:2], mixed[1:count // 2 * 2:2]
    margin = jnp.minimum(tallies[donor] - 1, bound - tallies[taker]) // 2
    margin = jnp.where((donor == ranking[0]) | (taker == ranking[0]) | (tallies[taker] == 0), 0, jnp.maximum(margin, 0))
    moved = jax.random.randint(jax.random.fold_in(own, 4), (count // 2,), 0, 1 << 20) % (margin + 1)
    tallies = tallies.at[donor].add(-moved).at[taker].add(moved)
    labels = jnp.searchsorted(jnp.cumsum(tallies), jnp.arange(rows * top), side="right").astype(jnp.int32)
    listing = labels.reshape(top, rows).T
    listing = listing[jax.random.permutation(jax.random.fold_in(own, 1), rows)]
    rotation = jax.random.randint(jax.random.fold_in(own, 2), (rows, 1), 0, top)
    return jnp.take_along_axis(listing, (jnp.arange(top)[None, :] + rotation) % top, axis=1)


def load_shares(number_of, total, most, skew, full):
    portions = [(1 << 20) // math.isqrt(grade ** skew) + 1 for grade in range(1, number_of + 1)]
    largest = most if full else min(most, max(-(-total // number_of), total * portions[0] // sum(portions)))
    least = 1 if total - largest >= number_of - 1 else 0
    holding, rest = [largest] + [least] * (number_of - 1), total - largest - least * (number_of - 1)
    while rest > 0:
        movable = [i for i in range(1, number_of) if holding[i] < largest] or [i for i in range(1, number_of) if holding[i] < most]
        whole, left = sum([portions[i] for i in movable]), rest
        for i in movable:
            addition = min(most - holding[i], max(1, left * portions[i] // whole), rest)
            holding[i] = holding[i] + addition
            rest = rest - addition
    return np.array(holding)


def setup_inputs(seed: int = 0) -> dict:
    key_list = jax.random.split(jax.random.key(seed), 10)
    src_table = draw_src_table(jax.random.fold_in(key_list[9], 71), 0)
    src_state = jnp.clip(jnp.exp(math.log(1.0) - 4.6051702 * jax.random.uniform(key_list[1], (SRC_ROWS,), jnp.float32) ** steps_of(key_list[1], (SRC_ROWS,), ((0, 32),), -0.2, 0.2)), 0.01, 1.0)
    tgt_table = draw_tgt_table(jax.random.fold_in(key_list[9], 71), 0)
    tgt_state = jnp.clip(jnp.exp(math.log(1.0) - 4.6051702 * jax.random.uniform(key_list[3], (TGT_ROWS,), jnp.float32) ** steps_of(key_list[3], (TGT_ROWS,), ((0, 32),), -0.2, 0.2)), 0.01, 1.0)
    pair_source = plant(jax.random.randint(key_list[4], (ROUNDS, PAIRS), 0, SRC_DEV), jax.random.fold_in(key_list[4], 1), 0, SRC_DEV - 1).astype(jnp.int32)
    pair_owner_keys = jax.random.split(jax.random.fold_in(key_list[5], 1), ROUNDS * PAIRS // PAIR_DEV)
    pair_owner_turns = jax.random.permutation(jax.random.fold_in(key_list[5], 3), ROUNDS * PAIRS // PAIR_DEV)
    pair_owner = jax.vmap(lambda own, number: deal_out(jax.random.fold_in(key_list[5], 2), own, number, PAIR_DEV, N_GRP, 1, CAP, 2))(pair_owner_keys, pair_owner_turns).reshape((ROUNDS, PAIRS, 1))
    pair_offset = plant(jax.random.randint(key_list[6], (ROUNDS, PAIRS), 0, TGT_DEV), jax.random.fold_in(key_list[6], 1), 0, TGT_DEV - 1).astype(jnp.int32)
    negatives = plant(jax.random.randint(key_list[7], (N_DOM, NEG), 0, N_GRP * TGT_DEV), jax.random.fold_in(key_list[7], 1), 0, (N_GRP * TGT_DEV) - 1).astype(jnp.int32)
    plan = jax.vmap(lambda own: jax.random.permutation(own, N_DOM))(jax.random.split(key_list[8], ROUNDS)).reshape((ROUNDS, N_DOM)).astype(jnp.int32)
    return dict(src_table=src_table, src_state=src_state, tgt_table=tgt_table, tgt_state=tgt_state, pair_source=pair_source, pair_owner=pair_owner, pair_offset=pair_offset, negatives=negatives, plan=plan)


LEARN = 0.1

def adagrad(emb_table, opt_state, grads):
    new_state = opt_state + lax.optimization_barrier(jnp.mean(grads * grads, axis=1))
    return (emb_table - LEARN * grads / jnp.sqrt(new_state)[:, None], new_state)

def reference(src_table, src_state, tgt_table, tgt_state, pair_source, pair_owner, pair_offset, negatives, plan):
    src_part_rows = N_GRP * SRC_DEV
    tgt_part_rows = N_GRP * TGT_DEV
    group_pairs = N_GRP * PAIR_DEV
    src_parts = src_table.reshape(N_DOM, src_part_rows, D)
    src_states = src_state.reshape(N_DOM, src_part_rows)
    tgt_parts = tgt_table.reshape(N_DOM, tgt_part_rows, D)
    tgt_states = tgt_state.reshape(N_DOM, tgt_part_rows)
    device_of_pair = (jnp.arange(group_pairs, dtype=jnp.int32) // PAIR_DEV).astype(jnp.int32)
    for round_index in range(ROUNDS):
        new_src, new_src_state = (src_parts, src_states)
        new_tgt, new_tgt_state = (tgt_parts, tgt_states)
        for domain in range(N_DOM):
            partition = plan[round_index, domain]
            begin = domain * group_pairs
            source_ids = device_of_pair * SRC_DEV + pair_source[round_index, begin:begin + group_pairs]
            target_ids = pair_owner[round_index, begin:begin + group_pairs, 0] * TGT_DEV + pair_offset[round_index, begin:begin + group_pairs]
            source_emb = src_parts[partition]
            target_emb = tgt_parts[domain]
            source_rows = source_emb[source_ids].astype(jnp.bfloat16)
            target_rows = target_emb[target_ids].astype(jnp.bfloat16)
            negative_rows = target_emb[negatives[domain]].astype(jnp.bfloat16)
            positive = lax.optimization_barrier(jnp.sum(source_rows.astype(jnp.float32) * target_rows.astype(jnp.float32), axis=1))
            negative = jnp.dot(source_rows, negative_rows.T, preferred_element_type=jnp.float32)
            score_max = jnp.maximum(lax.optimization_barrier(jnp.max(negative, axis=1)), positive)
            pos_exp = jnp.exp(positive - score_max)
            neg_exp = jnp.exp(negative - score_max[:, None])
            exp_total = pos_exp + lax.optimization_barrier(jnp.sum(neg_exp, axis=1))
            d_pos = pos_exp / exp_total - 1.0
            d_neg = (neg_exp / exp_total[:, None]).astype(jnp.bfloat16)
            source_grad = (d_pos[:, None] * target_rows.astype(jnp.float32) + jnp.dot(d_neg, negative_rows, preferred_element_type=jnp.float32)).astype(jnp.bfloat16)
            src_grads = jnp.zeros((src_part_rows, D), jnp.float32).at[source_ids].add(source_grad.astype(jnp.float32))
            tgt_grads = jnp.zeros((tgt_part_rows, D), jnp.float32).at[target_ids].add(d_pos[:, None] * source_rows.astype(jnp.float32))
            tgt_grads = tgt_grads.at[negatives[domain]].add(jnp.dot(d_neg.T, source_rows, preferred_element_type=jnp.float32))
            src_new, src_state_new = adagrad(source_emb, src_states[partition], src_grads)
            tgt_new, tgt_state_new = adagrad(target_emb, tgt_states[domain], tgt_grads)
            new_src = new_src.at[partition].set(src_new)
            new_src_state = new_src_state.at[partition].set(src_state_new)
            new_tgt = new_tgt.at[domain].set(tgt_new)
            new_tgt_state = new_tgt_state.at[domain].set(tgt_state_new)
        src_parts, src_states = (new_src, new_src_state)
        tgt_parts, tgt_states = (new_tgt, new_tgt_state)
    return (src_parts.reshape(SRC_ROWS, D), src_states.reshape(SRC_ROWS), tgt_parts.reshape(TGT_ROWS, D), tgt_states.reshape(TGT_ROWS))
```

```python
import functools

import jax
import jax.numpy as jnp
from jax import lax
from jax.experimental import pallas as pl
from jax.experimental.pallas import tpu as pltpu
from jax.sharding import PartitionSpec as P

LEARN = 0.1
LOW = -1e30
ROWS, STATS, SUMS, BACK, HOME, NAMES, GROUP = range(7)
NT = (((1,), (1,)), ((), ()))
TN = (((0,), (0,)), ((), ()))


def train_kernel(
    n_dom,
    n_grp,
    rounds,
    plan,
    negs,
    names,
    src_in,
    src_state_in,
    tgt_in,
    tgt_state_in,
    src,
    src_state,
    tgt,
    tgt_state,
    name_all,
    mult,
    tgt_bf,
    row_all,
    src_all,
    scores,
    pulls,
    counts,
    weights,
    stat_all,
    sum_all,
    back_out,
    back_all,
    home_all,
    send_sem,
    recv_sem,
):
    my_dom = lax.axis_index("dom")
    my_grp = lax.axis_index("grp")
    src_dev, width = src.shape
    tgt_dev = tgt.shape[0]
    tile = 256
    tiles = tgt_dev // tile
    src_part = n_grp * src_dev
    f32, bf16 = jnp.float32, jnp.bfloat16

    def peers(axis, body):
        size, me = (n_dom, my_dom) if axis == "dom" else (n_grp, my_grp)

        @pl.loop(1, size)
        def _(step):
            body(step, lax.rem(me + step, size))

    def copy(kind, r, axis, step, peer, source, target):
        return pltpu.make_async_remote_copy(
            src_ref=source,
            dst_ref=target,
            send_sem=send_sem.at[r, kind, step],
            recv_sem=recv_sem.at[r, kind, step],
            device_id={axis: peer},
            device_id_type=pl.DeviceIdType.MESH,
        )

    def spread(kind, r, axis, source, target):
        peers(axis, lambda step, peer: copy(kind, r, axis, step, peer, source, target).start())

    def gathered(kind, r, axis, source, target):
        peers(axis, lambda step, peer: copy(kind, r, axis, step, peer, source, target).wait())

    def rows_of(index):
        return pl.ds(pl.multiple_of(index * tile, tile), tile)

    def count_pairs(r):
        @pl.loop(0, n_grp)
        def _(g):
            source = name_all[g, r, 0:1, :]
            target = name_all[g, r, 1:2, :] - my_grp * tgt_dev
            pairs = source.shape[1]
            source_hot = jnp.where(
                lax.broadcasted_iota(jnp.int32, (src_dev, pairs), 0) == source, 1.0, 0.0
            ).astype(bf16)
            columns = pl.ds(pl.multiple_of(g * src_dev, src_dev), src_dev)

            @pl.loop(0, tiles)
            def _(i):
                target_hot = jnp.where(
                    lax.broadcasted_iota(jnp.int32, (tile, pairs), 0) == target - i * tile, 1.0, 0.0
                ).astype(bf16)
                counts[rows_of(i), columns] = lax.dot_general(
                    target_hot, source_hot, NT, preferred_element_type=f32
                ).astype(bf16)

    barrier = pltpu.get_barrier_semaphore()

    def greet(axis):
        def body(step, peer):
            pl.semaphore_signal(
                barrier, inc=1, device_id={axis: peer}, device_id_type=pl.DeviceIdType.MESH
            )

        peers(axis, body)

    greet("dom")
    greet("grp")
    row_all[0, my_dom] = src_in[...].astype(bf16)
    name_all[my_grp] = names[...]
    pl.semaphore_wait(barrier, n_dom + n_grp - 2)
    spread(NAMES, 0, "grp", name_all.at[my_grp], name_all.at[my_grp])
    spread(ROWS, 0, "dom", row_all.at[0, my_dom], row_all.at[0, my_dom])

    src[...] = src_in[...]
    src_state[...] = src_state_in[...]

    @pl.loop(0, tiles)
    def _(i):
        here = lax.broadcasted_iota(jnp.int32, (tile, negs.shape[1]), 0)
        wanted = negs[...] - (my_grp * tgt_dev + i * tile)
        mult[rows_of(i)] = jnp.sum(jnp.where(here == wanted, 1.0, 0.0), axis=1, keepdims=True)
        tgt[rows_of(i)] = tgt_in[rows_of(i)]
        tgt_bf[rows_of(i)] = tgt_in[rows_of(i)].astype(bf16)
        tgt_state[rows_of(i)] = tgt_state_in[rows_of(i)]

    gathered(NAMES, 0, "grp", name_all.at[my_grp], name_all.at[my_grp])
    count_pairs(0)

    @pl.loop(0, rounds)
    def _(r):
        gathered(ROWS, r, "dom", row_all.at[r, my_dom], row_all.at[r, my_dom])
        src_all[r, my_grp] = row_all[r, plan[r, my_dom]]
        mine = src_all.at[r, my_grp]
        spread(GROUP, r, "grp", mine, mine)
        gathered(GROUP, r, "grp", mine, mine)
        sources = src_all[r].reshape(src_part, width)

        def score(i, top):
            found = lax.dot_general(tgt_bf[rows_of(i)], sources, NT, preferred_element_type=f32)
            scores[rows_of(i)] = found
            named = jnp.where(mult[rows_of(i)] > 0, found, LOW)
            return jnp.maximum(top, jnp.max(named, axis=0, keepdims=True))

        top = lax.fori_loop(0, tiles, score, jnp.full((1, src_part), LOW, f32))

        def add_exp(i, total):
            many = mult[rows_of(i)]
            named = jnp.where(many > 0, scores[rows_of(i)], LOW)
            return total + jnp.sum(many * jnp.exp(named - top), axis=0, keepdims=True)

        total = lax.fori_loop(0, tiles, add_exp, jnp.zeros((1, src_part), f32))
        stat_all[r, my_grp, 0:1, :] = top
        stat_all[r, my_grp, 1:2, :] = total
        mine = stat_all.at[r, my_grp]
        spread(STATS, r, "grp", mine, mine)
        gathered(STATS, r, "grp", mine, mine)
        top = stat_all[r, 0, 0:1, :]
        for g in range(1, n_grp):
            top = jnp.maximum(top, stat_all[r, g, 0:1, :])
        total = jnp.zeros((1, src_part), f32)
        for g in range(n_grp):
            total += stat_all[r, g, 1:2, :] * jnp.exp(stat_all[r, g, 0:1, :] - top)
        log_total = jnp.log(total)
        part = 1.0 / total

        def pull(i, pulled):
            many = mult[rows_of(i)]
            found = scores[rows_of(i)]
            gap = (top - found) + log_total
            small = jnp.exp(-jnp.abs(gap))
            miss = jnp.where(gap >= 0, 1.0, small) / (1.0 + small)
            miss = miss * counts[rows_of(i)].astype(f32)
            pulls[rows_of(i)] = miss
            scores[rows_of(i)] = many * jnp.exp(jnp.where(many > 0, found, LOW) - top) * part
            return pulled + jnp.sum(miss, axis=0, keepdims=True)

        pulled = lax.fori_loop(0, tiles, pull, jnp.zeros((1, src_part), f32))
        sum_all[r, my_grp] = pulled
        mine = sum_all.at[r, my_grp]
        spread(SUMS, r, "grp", mine, mine)
        gathered(SUMS, r, "grp", mine, mine)
        pulled = sum_all[r, 0]
        for g in range(1, n_grp):
            pulled += sum_all[r, g]

        @pl.loop(0, tiles)
        def _(i):
            weights[rows_of(i)] = (pulled * scores[rows_of(i)] - pulls[rows_of(i)]).astype(bf16)

        both = 2 * src_dev
        pairs_of = n_grp // 2

        @pl.loop(0, pairs_of)
        def _(step):
            chip = lax.rem(my_grp // 2 + step, pairs_of)
            columns = pl.ds(pl.multiple_of(chip * both, both), both)
            grads = lax.dot_general(
                weights[:, columns], tgt_bf[...], TN, preferred_element_type=f32
            ).astype(bf16)
            for core in range(2):
                peer = chip * 2 + core
                back_out[r, peer] = grads[core * src_dev : (core + 1) * src_dev]

                @pl.when(peer != my_grp)
                def _():
                    copy(
                        BACK,
                        r,
                        "grp",
                        lax.rem(peer - my_grp + n_grp, n_grp),
                        peer,
                        back_out.at[r, peer],
                        back_all.at[r, my_grp],
                    ).start()

        @pl.loop(0, tiles)
        def _(i):
            grads = jnp.dot(weights[rows_of(i)], sources, preferred_element_type=f32)
            state = tgt_state[rows_of(i)] + jnp.sum(grads * grads, axis=1, keepdims=True) / width
            tgt_state[rows_of(i)] = state
            rows = tgt[rows_of(i)] - (LEARN * grads) / jnp.sqrt(state)
            tgt[rows_of(i)] = rows
            tgt_bf[rows_of(i)] = rows.astype(bf16)

        @pl.when(r + 1 < rounds)
        def _():
            count_pairs(r + 1)

        back_all[r, my_grp] = back_out[r, my_grp]
        peers(
            "grp",
            lambda step, peer: copy(
                BACK, r, "grp", step, peer, back_out.at[r, peer], back_all.at[r, my_grp]
            ).wait(),
        )
        grads = back_all[r, 0].astype(f32)
        for g in range(1, n_grp):
            grads += back_all[r, g].astype(f32)
        home_all[r, my_dom] = grads.astype(bf16)
        mine = home_all.at[r, my_dom]
        spread(HOME, r, "dom", mine, mine)
        gathered(HOME, r, "dom", mine, mine)
        trainer = jnp.int32(0)
        for d in range(n_dom):
            trainer = jnp.where(plan[r, d] == my_dom, d, trainer)
        grads = home_all[r, trainer].astype(f32)
        state = src_state[...] + jnp.sum(grads * grads, axis=1, keepdims=True) / width
        src_state[...] = state
        rows = src[...] - (LEARN * grads) / jnp.sqrt(state)
        src[...] = rows

        @pl.when(r + 1 < rounds)
        def _():
            row_all[r + 1, my_dom] = rows.astype(bf16)
            mine = row_all.at[r + 1, my_dom]
            spread(ROWS, r + 1, "dom", mine, mine)


def shards(
    n_dom,
    n_grp,
    src_table,
    src_state,
    tgt_table,
    tgt_state,
    pair_source,
    pair_owner,
    pair_offset,
    negatives,
    plan,
):
    rounds = plan.shape[0]
    src_dev, width = src_table.shape
    tgt_dev = tgt_table.shape[0]
    src_part = n_grp * src_dev
    f32, bf16 = jnp.float32, jnp.bfloat16
    names = jnp.stack([pair_source, pair_owner[:, :, 0] * tgt_dev + pair_offset], axis=1)
    vmem = pl.BlockSpec(memory_space=pltpu.VMEM)
    steps = max(n_dom, n_grp)
    new_src, new_src_state, new_tgt, new_tgt_state = pl.pallas_call(
        functools.partial(train_kernel, n_dom, n_grp, rounds),
        out_shape=(
            jax.ShapeDtypeStruct((src_dev, width), f32),
            jax.ShapeDtypeStruct((src_dev, 1), f32),
            jax.ShapeDtypeStruct((tgt_dev, width), f32),
            jax.ShapeDtypeStruct((tgt_dev, 1), f32),
        ),
        in_specs=[pl.BlockSpec(memory_space=pltpu.SMEM)] + [vmem] * 6,
        out_specs=[vmem] * 4,
        scratch_shapes=[
            pltpu.VMEM((n_grp,) + names.shape, jnp.int32),
            pltpu.VMEM((tgt_dev, 1), f32),
            pltpu.VMEM((tgt_dev, width), bf16),
            pltpu.VMEM((rounds, n_dom, src_dev, width), bf16),
            pltpu.VMEM((rounds, n_grp, src_dev, width), bf16),
            pltpu.VMEM((tgt_dev, src_part), f32),
            pltpu.VMEM((tgt_dev, src_part), f32),
            pltpu.VMEM((tgt_dev, src_part), bf16),
            pltpu.VMEM((tgt_dev, src_part), bf16),
            pltpu.VMEM((rounds, n_grp, 2, src_part), f32),
            pltpu.VMEM((rounds, n_grp, 1, src_part), f32),
            pltpu.VMEM((rounds, n_grp, src_dev, width), bf16),
            pltpu.VMEM((rounds, n_grp, src_dev, width), bf16),
            pltpu.VMEM((rounds, n_dom, src_dev, width), bf16),
            pltpu.SemaphoreType.DMA((rounds, 7, steps)),
            pltpu.SemaphoreType.DMA((rounds, 7, steps)),
        ],
        compiler_params=pltpu.CompilerParams(
            collective_id=0, has_side_effects=True, vmem_limit_bytes=56 * 1024 * 1024
        ),
        name="train",
    )(
        plan,
        negatives,
        names,
        src_table,
        src_state[:, None],
        tgt_table,
        tgt_state[:, None],
    )
    return (new_src, new_src_state[:, 0], new_tgt, new_tgt_state[:, 0])


def solution(mesh):
    return jax.shard_map(
        functools.partial(shards, mesh.shape["dom"], mesh.shape["grp"]),
        mesh=mesh,
        in_specs=(
            P(("dom", "grp"), None),
            P(("dom", "grp")),
            P(("dom", "grp"), None),
            P(("dom", "grp")),
            P(None, ("dom", "grp")),
            P(None, ("dom", "grp"), None),
            P(None, ("dom", "grp")),
            P("dom", None),
            P(),
        ),
        out_specs=(
            P(("dom", "grp"), None),
            P(("dom", "grp")),
            P(("dom", "grp"), None),
            P(("dom", "grp")),
        ),
        check_vma=False,
    )
```

```python
import functools

import jax
import jax.numpy as jnp
from jax import lax
from jax.experimental import pallas as pl
from jax.experimental.pallas import tpu as pltpu
from jax.sharding import PartitionSpec as P

LEARN = 0.1
LOW = -1e30
ROWS, STATS, SUMS, BACK, HOME, NAMES, GROUP, PASS, PART, FULL, STATE, KINDS = range(12)
NT = (((1,), (1,)), ((), ()))


def train_kernel(
    n_dom,
    n_grp,
    rounds,
    plan,
    negs,
    pair_source,
    pair_owner,
    pair_offset,
    src_in,
    src_state_in,
    tgt_in,
    tgt_state_in,
    src,
    src_state,
    tgt,
    tgt_state,
    name_all,
    mult,
    tgt_bf,
    tgt_rows,
    row_all,
    full_all,
    state_all,
    src_all,
    scores,
    pulls,
    counts,
    weights,
    stat_all,
    sum_all,
    part_own,
    part_got,
    back_out,
    back_all,
    home_all,
    send_sem,
    recv_sem,
):
    my_dom = lax.axis_index("dom")
    my_grp = lax.axis_index("grp")
    chips = n_grp // 2
    my_chip, my_core = my_grp // 2, lax.rem(my_grp, 2)
    sibling = my_chip * 2 + 1 - my_core
    width, src_dev = src.shape
    tgt_dev = tgt.shape[1]
    tile = 256
    tiles = tgt_dev // tile
    both = 2 * src_dev
    src_part = n_grp * src_dev
    f32, bf16 = jnp.float32, jnp.bfloat16

    def peers(axis, body):
        size, me = (n_dom, my_dom) if axis == "dom" else (n_grp, my_grp)

        @pl.loop(1, size)
        def _(step):
            body(step, lax.rem(me + step, size))

    def copy(kind, r, axis, step, peer, source, target):
        return pltpu.make_async_remote_copy(
            src_ref=source,
            dst_ref=target,
            send_sem=send_sem.at[r, kind, step],
            recv_sem=recv_sem.at[r, kind, step],
            device_id={axis: peer},
            device_id_type=pl.DeviceIdType.MESH,
        )

    def spread(kind, r, axis, ref):
        peers(axis, lambda step, peer: copy(kind, r, axis, step, peer, ref, ref).start())

    def gathered(kind, r, axis, ref):
        peers(axis, lambda step, peer: copy(kind, r, axis, step, peer, ref, ref).wait())

    def span(index, size):
        return pl.ds(pl.multiple_of(index * size, size), size)

    def rows_of(index):
        return span(index, tile)

    def count_pairs(r, first, last):
        @pl.loop(first, last)
        def _(g):
            source = name_all[g, 0, pl.ds(r, 1), :]
            target = name_all[g, 1, pl.ds(r, 1), :] - my_grp * tgt_dev
            pairs = source.shape[1]
            source_hot = jnp.where(
                lax.broadcasted_iota(jnp.int32, (src_dev, pairs), 0) == source, 1.0, 0.0
            ).astype(bf16)

            @pl.loop(0, tiles)
            def _(i):
                target_hot = jnp.where(
                    lax.broadcasted_iota(jnp.int32, (tile, pairs), 0) == target - i * tile, 1.0, 0.0
                ).astype(bf16)
                counts[rows_of(i), span(g, src_dev)] = lax.dot_general(
                    target_hot, source_hot, NT, preferred_element_type=f32
                ).astype(bf16)

    barrier = pltpu.get_barrier_semaphore()

    def greet(axis):
        def body(step, peer):
            pl.semaphore_signal(
                barrier, inc=1, device_id={axis: peer}, device_id_type=pl.DeviceIdType.MESH
            )

        peers(axis, body)

    greet("dom")
    greet("grp")
    row_all[my_dom] = src_in[...].astype(bf16)
    full_all[my_dom] = src_in[...]
    state_all[my_dom] = src_state_in[...]
    name_all[my_grp, 0] = pair_source[...]
    name_all[my_grp, 1] = pair_owner[...] * tgt_dev + pair_offset[...]
    pl.semaphore_wait(barrier, n_dom + n_grp - 2)
    spread(ROWS, 0, "dom", row_all.at[my_dom])
    spread(NAMES, 0, "grp", name_all.at[my_grp])

    @pl.loop(0, tiles)
    def _(i):
        here = lax.broadcasted_iota(jnp.int32, (tile, negs.shape[1]), 0)
        wanted = negs[...] - (my_grp * tgt_dev + i * tile)
        mult[rows_of(i)] = jnp.sum(jnp.where(here == wanted, 1.0, 0.0), axis=1, keepdims=True)
        rows = tgt_in[:, rows_of(i)]
        tgt[:, rows_of(i)] = rows
        tgt_bf[:, rows_of(i)] = rows.astype(bf16)
        tgt_rows[rows_of(i)] = rows.T.astype(bf16)

    tgt_state[...] = tgt_state_in[...]
    gathered(NAMES, 0, "grp", name_all.at[my_grp])
    count_pairs(0, 0, chips)
    gathered(ROWS, 0, "dom", row_all.at[my_dom])
    src_all[0, :, span(my_grp, src_dev)] = row_all[plan[0, my_dom]]

    @pl.loop(0, rounds)
    def _(r):
        def column(index):
            return src_all.at[r, :, span(index, src_dev)]

        def to_chip(step):
            peer = lax.rem(my_chip + step, chips) * 2 + my_core
            return copy(GROUP, r, "grp", step, peer, column(my_grp), column(my_grp))

        def to_sibling(step):
            held = lax.rem(my_chip - step + chips, chips) * 2 + my_core
            return copy(PASS, r, "grp", step, sibling, column(held), column(held))

        for step in range(1, chips):
            to_chip(step).start()
        to_sibling(0).start()

        @pl.when(r == 0)
        def _():
            spread(FULL, 0, "dom", full_all.at[my_dom])
            spread(STATE, 0, "dom", state_all.at[my_dom])

        count_pairs(r, chips, n_grp)

        def score_chip(chip):
            columns = span(chip, both)

            def score(i, top):
                found = jnp.dot(
                    tgt_rows[rows_of(i)], src_all[r, :, columns], preferred_element_type=f32
                )
                scores[rows_of(i), columns] = found
                named = jnp.where(mult[rows_of(i)] > 0, found, LOW)
                return jnp.maximum(top, jnp.max(named, axis=0, keepdims=True))

            top = lax.fori_loop(0, tiles, score, jnp.full((1, both), LOW, f32))

            def add_exp(i, total):
                many = mult[rows_of(i)]
                named = jnp.where(many > 0, scores[rows_of(i), columns], LOW)
                return total + jnp.sum(many * jnp.exp(named - top), axis=0, keepdims=True)

            total = lax.fori_loop(0, tiles, add_exp, jnp.zeros((1, both), f32))
            stat_all[r, my_grp, 0:1, columns] = top
            stat_all[r, my_grp, 1:2, columns] = total

        for step in range(1, chips + 1):
            if step < chips:
                to_chip(step).wait()
                to_sibling(step).start()
            to_sibling(step - 1).wait()
            score_chip(lax.rem(my_chip - (step - 1) + chips, chips))

        spread(STATS, r, "grp", stat_all.at[r, my_grp])
        gathered(STATS, r, "grp", stat_all.at[r, my_grp])
        top = stat_all[r, 0, 0:1, :]
        for g in range(1, n_grp):
            top = jnp.maximum(top, stat_all[r, g, 0:1, :])
        total = jnp.zeros((1, src_part), f32)
        for g in range(n_grp):
            total += stat_all[r, g, 1:2, :] * jnp.exp(stat_all[r, g, 0:1, :] - top)
        log_total = jnp.log(total)
        part = 1.0 / total

        def pull(i, pulled):
            found = scores[rows_of(i)]
            gap = (top - found) + log_total
            small = jnp.exp(-jnp.abs(gap))
            miss = jnp.where(gap >= 0, 1.0, small) / (1.0 + small)
            miss = miss * counts[rows_of(i)].astype(f32)
            pulls[rows_of(i)] = miss
            return pulled + jnp.sum(miss, axis=0, keepdims=True)

        pulled = lax.fori_loop(0, tiles, pull, jnp.zeros((1, src_part), f32))
        sum_all[r, my_grp] = pulled
        spread(SUMS, r, "grp", sum_all.at[r, my_grp])

        @pl.loop(0, tiles)
        def _(i):
            many = mult[rows_of(i)]
            named = jnp.where(many > 0, scores[rows_of(i)], LOW)
            scores[rows_of(i)] = many * jnp.exp(named - top) * part

        gathered(SUMS, r, "grp", sum_all.at[r, my_grp])
        pulled = sum_all[r, 0]
        for g in range(1, n_grp):
            pulled += sum_all[r, g]

        @pl.loop(0, tiles)
        def _(i):
            weights[rows_of(i)] = (pulled * scores[rows_of(i)] - pulls[rows_of(i)]).astype(bf16)

        mine, other = span(my_core, src_dev), span(1 - my_core, src_dev)

        def give_part(step):
            return copy(
                PART, r, "grp", step, sibling, part_own.at[r, step, :, other], part_got.at[r, step]
            )

        def give_back(step):
            peer = lax.rem(my_chip + step, chips) * 2 + my_core
            return copy(BACK, r, "grp", step, peer, back_out.at[r, step], back_all.at[r, step])

        def chip_sum(step):
            give_part(step).wait()
            return part_own[r, step, :, mine].astype(f32) + part_got[r, step].astype(f32)

        for turn in range(1, chips + 1):
            step = turn % chips
            columns = span(lax.rem(my_chip + step, chips), both)
            part_own[r, step] = jnp.dot(
                tgt_bf[...], weights[:, columns], preferred_element_type=f32
            ).astype(bf16)
            give_part(step).start()
            if turn > 1:
                back_out[r, turn - 1] = chip_sum(turn - 1).astype(bf16)
                give_back(turn - 1).start()

        @pl.loop(0, tiles)
        def _(i):
            grads = lax.dot_general(
                src_all[r], weights[rows_of(i)], NT, preferred_element_type=f32
            )
            state = tgt_state[:, rows_of(i)] + jnp.sum(grads * grads, axis=0, keepdims=True) / width
            tgt_state[:, rows_of(i)] = state
            rows = tgt[:, rows_of(i)] - (LEARN * grads) / jnp.sqrt(state)
            tgt[:, rows_of(i)] = rows

            @pl.when(r + 1 < rounds)
            def _():
                tgt_bf[:, rows_of(i)] = rows.astype(bf16)
                tgt_rows[rows_of(i)] = rows.T.astype(bf16)

        grads = chip_sum(0)
        for step in range(1, chips):
            give_back(step).wait()
            grads += back_all[r, step].astype(f32)
        home_all[r, my_dom] = grads.astype(bf16)
        spread(HOME, r, "dom", home_all.at[r, my_dom])

        @pl.when(r + 1 < rounds)
        def _():
            count_pairs(r + 1, 0, chips)

        @pl.when(r == 0)
        def _():
            gathered(FULL, 0, "dom", full_all.at[my_dom])
            gathered(STATE, 0, "dom", state_all.at[my_dom])

        gathered(HOME, r, "dom", home_all.at[r, my_dom])

        @pl.loop(0, n_dom)
        def _(p):
            grads = home_all[r, 0].astype(f32)
            for d in range(1, n_dom):
                grads = jnp.where(plan[r, d] == p, home_all[r, d].astype(f32), grads)
            state = state_all[p] + jnp.sum(grads * grads, axis=0, keepdims=True) / width
            state_all[p] = state
            full_all[p] = full_all[p] - (LEARN * grads) / jnp.sqrt(state)

        @pl.when(r + 1 < rounds)
        def _():
            src_all[r + 1, :, span(my_grp, src_dev)] = full_all[plan[r + 1, my_dom]].astype(bf16)

    src[...] = full_all[my_dom]
    src_state[...] = state_all[my_dom]


def shards(
    n_dom,
    n_grp,
    src_table,
    src_state,
    tgt_table,
    tgt_state,
    pair_source,
    pair_owner,
    pair_offset,
    negatives,
    plan,
):
    rounds, pairs = pair_source.shape
    src_dev, width = src_table.shape
    tgt_dev = tgt_table.shape[0]
    src_part = n_grp * src_dev
    chips = n_grp // 2
    f32, bf16 = jnp.float32, jnp.bfloat16
    vmem = pl.BlockSpec(memory_space=pltpu.VMEM)
    steps = max(n_dom, n_grp)
    new_src, new_src_state, new_tgt, new_tgt_state = pl.pallas_call(
        functools.partial(train_kernel, n_dom, n_grp, rounds),
        out_shape=(
            jax.ShapeDtypeStruct((width, src_dev), f32),
            jax.ShapeDtypeStruct((1, src_dev), f32),
            jax.ShapeDtypeStruct((width, tgt_dev), f32),
            jax.ShapeDtypeStruct((1, tgt_dev), f32),
        ),
        in_specs=[pl.BlockSpec(memory_space=pltpu.SMEM)] + [vmem] * 8,
        out_specs=[vmem] * 4,
        scratch_shapes=[
            pltpu.VMEM((n_grp, 2, rounds, pairs), jnp.int32),
            pltpu.VMEM((tgt_dev, 1), f32),
            pltpu.VMEM((width, tgt_dev), bf16),
            pltpu.VMEM((tgt_dev, width), bf16),
            pltpu.VMEM((n_dom, width, src_dev), bf16),
            pltpu.VMEM((n_dom, width, src_dev), f32),
            pltpu.VMEM((n_dom, 1, src_dev), f32),
            pltpu.VMEM((rounds, width, src_part), bf16),
            pltpu.VMEM((tgt_dev, src_part), f32),
            pltpu.VMEM((tgt_dev, src_part), f32),
            pltpu.VMEM((tgt_dev, src_part), bf16),
            pltpu.VMEM((tgt_dev, src_part), bf16),
            pltpu.VMEM((rounds, n_grp, 2, src_part), f32),
            pltpu.VMEM((rounds, n_grp, 1, src_part), f32),
            pltpu.VMEM((rounds, chips, width, 2 * src_dev), bf16),
            pltpu.VMEM((rounds, chips, width, src_dev), bf16),
            pltpu.VMEM((rounds, chips, width, src_dev), bf16),
            pltpu.VMEM((rounds, chips, width, src_dev), bf16),
            pltpu.VMEM((rounds, n_dom, width, src_dev), bf16),
            pltpu.SemaphoreType.DMA((rounds, KINDS, steps)),
            pltpu.SemaphoreType.DMA((rounds, KINDS, steps)),
        ],
        compiler_params=pltpu.CompilerParams(
            collective_id=0, has_side_effects=True, vmem_limit_bytes=56 * 1024 * 1024
        ),
        name="train",
    )(
        plan,
        negatives,
        pair_source,
        pair_owner[:, :, 0],
        pair_offset,
        src_table.T,
        src_state[None, :],
        tgt_table.T,
        tgt_state[None, :],
    )
    return (new_src.T, new_src_state[0], new_tgt.T, new_tgt_state[0])


def solution(mesh):
    return jax.shard_map(
        functools.partial(shards, mesh.shape["dom"], mesh.shape["grp"]),
        mesh=mesh,
        in_specs=(
            P(("dom", "grp"), None),
            P(("dom", "grp")),
            P(("dom", "grp"), None),
            P(("dom", "grp")),
            P(None, ("dom", "grp")),
            P(None, ("dom", "grp"), None),
            P(None, ("dom", "grp")),
            P("dom", None),
            P(),
        ),
        out_specs=(
            P(("dom", "grp"), None),
            P(("dom", "grp")),
            P(("dom", "grp"), None),
            P(("dom", "grp")),
        ),
        check_vma=False,
    )
```

```python
import functools

import jax
import jax.numpy as jnp
from jax import lax
from jax.experimental import pallas as pl
from jax.experimental.pallas import tpu as pltpu
from jax.sharding import PartitionSpec as P

LEARN = 0.1
LOW = -1e30
ROWS, STATS, SUMS, BACK, HOME, NAMES, GROUP, PASS, PART, FULL, STATE, KINDS = range(12)
NT = (((1,), (1,)), ((), ()))


def train_kernel(
    n_dom,
    n_grp,
    rounds,
    plan,
    negs,
    pair_source,
    pair_owner,
    pair_offset,
    src_in,
    src_state_in,
    tgt_in,
    tgt_state_in,
    src,
    src_state,
    tgt,
    tgt_state,
    name_all,
    mult,
    tgt_bf,
    tgt_rows,
    row_all,
    full_all,
    state_all,
    src_all,
    scores,
    exps,
    pulls,
    counts,
    exp_grads,
    pull_grads,
    scaled,
    stat_all,
    sum_all,
    part_own,
    part_got,
    back_out,
    back_all,
    home_all,
    send_sem,
    recv_sem,
):
    my_dom = lax.axis_index("dom")
    my_grp = lax.axis_index("grp")
    chips = n_grp // 2
    my_chip, my_core = my_grp // 2, lax.rem(my_grp, 2)
    sibling = my_chip * 2 + 1 - my_core
    width, src_dev = src.shape
    tgt_dev = tgt.shape[1]
    tile = 256
    tiles = tgt_dev // tile
    both = 2 * src_dev
    src_part = n_grp * src_dev
    f32, bf16 = jnp.float32, jnp.bfloat16

    def peers(axis, body):
        size, me = (n_dom, my_dom) if axis == "dom" else (n_grp, my_grp)

        @pl.loop(1, size)
        def _(step):
            body(step, lax.rem(me + step, size))

    def copy(kind, r, axis, step, peer, source, target):
        return pltpu.make_async_remote_copy(
            src_ref=source,
            dst_ref=target,
            send_sem=send_sem.at[r, kind, step],
            recv_sem=recv_sem.at[r, kind, step],
            device_id={axis: peer},
            device_id_type=pl.DeviceIdType.MESH,
        )

    def spread(kind, r, axis, ref):
        peers(axis, lambda step, peer: copy(kind, r, axis, step, peer, ref, ref).start())

    def gathered(kind, r, axis, ref):
        peers(axis, lambda step, peer: copy(kind, r, axis, step, peer, ref, ref).wait())

    def span(index, size):
        return pl.ds(pl.multiple_of(index * size, size), size)

    def rows_of(index):
        return span(index, tile)

    def count_pairs(r, first, last):
        @pl.loop(first, last)
        def _(g):
            source = name_all[g, 0, pl.ds(r, 1), :]
            target = name_all[g, 1, pl.ds(r, 1), :] - my_grp * tgt_dev
            pairs = source.shape[1]
            source_hot = jnp.where(
                lax.broadcasted_iota(jnp.int32, (src_dev, pairs), 0) == source, 1.0, 0.0
            ).astype(bf16)

            @pl.loop(0, tiles)
            def _(i):
                target_hot = jnp.where(
                    lax.broadcasted_iota(jnp.int32, (tile, pairs), 0) == target - i * tile, 1.0, 0.0
                ).astype(bf16)
                counts[rows_of(i), span(g, src_dev)] = lax.dot_general(
                    target_hot, source_hot, NT, preferred_element_type=f32
                ).astype(bf16)

    barrier = pltpu.get_barrier_semaphore()

    def greet(axis):
        def body(step, peer):
            pl.semaphore_signal(
                barrier, inc=1, device_id={axis: peer}, device_id_type=pl.DeviceIdType.MESH
            )

        peers(axis, body)

    greet("dom")
    greet("grp")
    row_all[my_dom] = src_in[...].astype(bf16)
    full_all[my_dom] = src_in[...]
    state_all[my_dom] = src_state_in[...]
    name_all[my_grp, 0] = pair_source[...]
    for r in range(rounds):
        name_all[my_grp, 1, r : r + 1] = pair_owner[r] * tgt_dev + pair_offset[r : r + 1]
    pl.semaphore_wait(barrier, n_dom + n_grp - 2)
    spread(ROWS, 0, "dom", row_all.at[my_dom])
    spread(NAMES, 0, "grp", name_all.at[my_grp])

    @pl.loop(0, tiles)
    def _(i):
        here = lax.broadcasted_iota(jnp.int32, (tile, negs.shape[1]), 0)
        wanted = negs[...] - (my_grp * tgt_dev + i * tile)
        mult[rows_of(i)] = jnp.sum(jnp.where(here == wanted, 1.0, 0.0), axis=1, keepdims=True)
        rows = tgt_in[:, rows_of(i)]
        tgt[:, rows_of(i)] = rows
        tgt_bf[:, rows_of(i)] = rows.astype(bf16)
        tgt_rows[rows_of(i)] = rows.T.astype(bf16)

    tgt_state[...] = tgt_state_in[...]
    gathered(NAMES, 0, "grp", name_all.at[my_grp])
    count_pairs(0, 0, chips)
    gathered(ROWS, 0, "dom", row_all.at[my_dom])
    src_all[0, :, span(my_grp, src_dev)] = row_all[plan[0, my_dom]]

    @pl.loop(0, rounds)
    def _(r):
        def column(index):
            return src_all.at[r, :, span(index, src_dev)]

        def to_chip(step):
            peer = lax.rem(my_chip + step, chips) * 2 + my_core
            return copy(GROUP, r, "grp", step, peer, column(my_grp), column(my_grp))

        def to_sibling(step):
            held = lax.rem(my_chip - step + chips, chips) * 2 + my_core
            return copy(PASS, r, "grp", step, sibling, column(held), column(held))

        for step in range(1, chips):
            to_chip(step).start()
        to_sibling(0).start()

        @pl.when(r == 0)
        def _():
            spread(FULL, 0, "dom", full_all.at[my_dom])
            spread(STATE, 0, "dom", state_all.at[my_dom])

        count_pairs(r, chips, n_grp)

        def score_chip(chip):
            columns = span(chip, both)

            def score(i, top):
                found = jnp.dot(
                    tgt_rows[rows_of(i)], src_all[r, :, columns], preferred_element_type=f32
                )
                scores[rows_of(i), columns] = found
                named = jnp.where(mult[rows_of(i)] > 0, found, LOW)
                return jnp.maximum(top, jnp.max(named, axis=0, keepdims=True))

            top = lax.fori_loop(0, tiles, score, jnp.full((1, both), LOW, f32))

            def add_exp(i, total):
                many = mult[rows_of(i)]
                named = jnp.where(many > 0, scores[rows_of(i), columns], LOW)
                grown = many * jnp.exp(named - top)
                exps[rows_of(i), columns] = grown.astype(bf16)
                return total + jnp.sum(grown, axis=0, keepdims=True)

            total = lax.fori_loop(0, tiles, add_exp, jnp.zeros((1, both), f32))
            stat_all[r, my_grp, 0:1, columns] = top
            stat_all[r, my_grp, 1:2, columns] = total

        for step in range(1, chips + 1):
            if step < chips:
                to_chip(step).wait()
                to_sibling(step).start()
            to_sibling(step - 1).wait()
            score_chip(lax.rem(my_chip - (step - 1) + chips, chips))

        spread(STATS, r, "grp", stat_all.at[r, my_grp])

        @pl.loop(0, chips)
        def _(chip):
            columns = span(chip, both)
            exp_grads[:, columns] = jnp.dot(
                tgt_bf[...], exps[:, columns], preferred_element_type=f32
            )

        gathered(STATS, r, "grp", stat_all.at[r, my_grp])
        top = stat_all[r, 0, 0:1, :]
        for g in range(1, n_grp):
            top = jnp.maximum(top, stat_all[r, g, 0:1, :])
        total = jnp.zeros((1, src_part), f32)
        for g in range(n_grp):
            total += stat_all[r, g, 1:2, :] * jnp.exp(stat_all[r, g, 0:1, :] - top)
        log_total = jnp.log(total)
        part = jnp.exp(stat_all[r, my_grp, 0:1, :] - top) / total

        def pull(i, pulled):
            gap = (scores[rows_of(i)] - top) - log_total
            miss = pl.reciprocal(1.0 + jnp.exp(jnp.minimum(gap, 80.0)), approx=True)
            miss = miss * counts[rows_of(i)].astype(f32)
            pulls[rows_of(i)] = miss.astype(bf16)
            return pulled + jnp.sum(miss, axis=0, keepdims=True)

        pulled = lax.fori_loop(0, tiles, pull, jnp.zeros((1, src_part), f32))
        sum_all[r, my_grp] = pulled
        spread(SUMS, r, "grp", sum_all.at[r, my_grp])

        @pl.loop(0, chips)
        def _(chip):
            columns = span(chip, both)
            pull_grads[:, columns] = jnp.dot(
                tgt_bf[...], pulls[:, columns], preferred_element_type=f32
            )

        gathered(SUMS, r, "grp", sum_all.at[r, my_grp])
        pulled = sum_all[r, 0]
        for g in range(1, n_grp):
            pulled += sum_all[r, g]
        sum_all[r, my_grp] = pulled * part
        factor = sum_all.at[r, my_grp]

        mine, other = span(my_core, src_dev), span(1 - my_core, src_dev)

        def give_part(step):
            return copy(
                PART, r, "grp", step, sibling, part_own.at[r, step, :, other], part_got.at[r, step]
            )

        def give_back(step):
            peer = lax.rem(my_chip + step, chips) * 2 + my_core
            return copy(BACK, r, "grp", step, peer, back_out.at[r, step], back_all.at[r, step])

        def chip_sum(step):
            give_part(step).wait()
            return part_own[r, step, :, mine].astype(f32) + part_got[r, step].astype(f32)

        for turn in range(1, chips + 1):
            step = turn % chips
            columns = span(lax.rem(my_chip + step, chips), both)
            part_own[r, step] = (
                exp_grads[:, columns] * factor[:, columns] - pull_grads[:, columns]
            ).astype(bf16)
            give_part(step).start()
            if turn > 1:
                back_out[r, turn - 1] = chip_sum(turn - 1).astype(bf16)
                give_back(turn - 1).start()

        scaled[...] = (src_all[r].astype(f32) * factor[...]).astype(bf16)

        @pl.loop(0, tiles)
        def _(i):
            grads = lax.dot_general(
                scaled[...], exps[rows_of(i)], NT, preferred_element_type=f32
            ) - lax.dot_general(src_all[r], pulls[rows_of(i)], NT, preferred_element_type=f32)
            state = tgt_state[:, rows_of(i)] + jnp.sum(grads * grads, axis=0, keepdims=True) / width
            tgt_state[:, rows_of(i)] = state
            rows = tgt[:, rows_of(i)] - (LEARN * grads) / jnp.sqrt(state)
            tgt[:, rows_of(i)] = rows

            @pl.when(r + 1 < rounds)
            def _():
                tgt_bf[:, rows_of(i)] = rows.astype(bf16)
                tgt_rows[rows_of(i)] = rows.T.astype(bf16)

        grads = chip_sum(0)
        for step in range(1, chips):
            give_back(step).wait()
            grads += back_all[r, step].astype(f32)
        home_all[r, my_dom] = grads.astype(bf16)
        spread(HOME, r, "dom", home_all.at[r, my_dom])

        @pl.when(r + 1 < rounds)
        def _():
            count_pairs(r + 1, 0, chips)

        @pl.when(r == 0)
        def _():
            gathered(FULL, 0, "dom", full_all.at[my_dom])
            gathered(STATE, 0, "dom", state_all.at[my_dom])

        gathered(HOME, r, "dom", home_all.at[r, my_dom])

        @pl.loop(0, n_dom)
        def _(p):
            grads = home_all[r, 0].astype(f32)
            for d in range(1, n_dom):
                grads = jnp.where(plan[r, d] == p, home_all[r, d].astype(f32), grads)
            state = state_all[p] + jnp.sum(grads * grads, axis=0, keepdims=True) / width
            state_all[p] = state
            full_all[p] = full_all[p] - (LEARN * grads) / jnp.sqrt(state)

        @pl.when(r + 1 < rounds)
        def _():
            src_all[r + 1, :, span(my_grp, src_dev)] = full_all[plan[r + 1, my_dom]].astype(bf16)

    src[...] = full_all[my_dom]
    src_state[...] = state_all[my_dom]


def hand_out(*refs):
    sources, targets, sems = refs[:4], refs[4:8], refs[8]
    copies = [
        pltpu.make_async_copy(source, target, sems.at[i])
        for i, (source, target) in enumerate(zip(sources, targets))
    ]
    for each in copies:
        each.start()
    for each in copies:
        each.wait()


def shards(
    n_dom,
    n_grp,
    src_table,
    src_state,
    tgt_table,
    tgt_state,
    pair_source,
    pair_owner,
    pair_offset,
    negatives,
    plan,
):
    rounds, pairs = pair_source.shape
    src_dev, width = src_table.shape
    tgt_dev = tgt_table.shape[0]
    src_part = n_grp * src_dev
    chips = n_grp // 2
    f32, bf16 = jnp.float32, jnp.bfloat16
    vmem = pl.BlockSpec(memory_space=pltpu.VMEM)
    steps = max(n_dom, n_grp)
    trained = pl.pallas_call(
        functools.partial(train_kernel, n_dom, n_grp, rounds),
        out_shape=(
            jax.ShapeDtypeStruct((width, src_dev), f32),
            jax.ShapeDtypeStruct((1, src_dev), f32),
            jax.ShapeDtypeStruct((width, tgt_dev), f32),
            jax.ShapeDtypeStruct((1, tgt_dev), f32),
        ),
        in_specs=[pl.BlockSpec(memory_space=pltpu.SMEM)] + [vmem] * 8,
        out_specs=[vmem] * 4,
        scratch_shapes=[
            pltpu.VMEM((n_grp, 2, rounds, pairs), jnp.int32),
            pltpu.VMEM((tgt_dev, 1), f32),
            pltpu.VMEM((width, tgt_dev), bf16),
            pltpu.VMEM((tgt_dev, width), bf16),
            pltpu.VMEM((n_dom, width, src_dev), bf16),
            pltpu.VMEM((n_dom, width, src_dev), f32),
            pltpu.VMEM((n_dom, 1, src_dev), f32),
            pltpu.VMEM((rounds, width, src_part), bf16),
            pltpu.VMEM((tgt_dev, src_part), f32),
            pltpu.VMEM((tgt_dev, src_part), bf16),
            pltpu.VMEM((tgt_dev, src_part), bf16),
            pltpu.VMEM((tgt_dev, src_part), bf16),
            pltpu.VMEM((width, src_part), f32),
            pltpu.VMEM((width, src_part), f32),
            pltpu.VMEM((width, src_part), bf16),
            pltpu.VMEM((rounds, n_grp, 2, src_part), f32),
            pltpu.VMEM((rounds, n_grp, 1, src_part), f32),
            pltpu.VMEM((rounds, chips, width, 2 * src_dev), bf16),
            pltpu.VMEM((rounds, chips, width, src_dev), bf16),
            pltpu.VMEM((rounds, chips, width, src_dev), bf16),
            pltpu.VMEM((rounds, chips, width, src_dev), bf16),
            pltpu.VMEM((rounds, n_dom, width, src_dev), bf16),
            pltpu.SemaphoreType.DMA((rounds, KINDS, steps)),
            pltpu.SemaphoreType.DMA((rounds, KINDS, steps)),
        ],
        compiler_params=pltpu.CompilerParams(
            collective_id=0, has_side_effects=True, vmem_limit_bytes=56 * 1024 * 1024
        ),
        name="train",
    )(
        plan,
        negatives,
        pair_source,
        pair_owner.transpose(0, 2, 1),
        pair_offset,
        src_table.T,
        src_state[None, :],
        tgt_table.T,
        tgt_state[None, :],
    )
    anywhere = pl.BlockSpec(memory_space=pl.ANY)
    new_src, new_src_state, new_tgt, new_tgt_state = pl.pallas_call(
        hand_out,
        out_shape=[jax.ShapeDtypeStruct(x.shape, x.dtype) for x in trained],
        in_specs=[anywhere] * 4,
        out_specs=[anywhere] * 4,
        scratch_shapes=[pltpu.SemaphoreType.DMA((4,))],
        name="hand_out",
    )(*trained)
    return (new_src.T, new_src_state[0], new_tgt.T, new_tgt_state[0])


def solution(mesh):
    return jax.shard_map(
        functools.partial(shards, mesh.shape["dom"], mesh.shape["grp"]),
        mesh=mesh,
        in_specs=(
            P(("dom", "grp"), None),
            P(("dom", "grp")),
            P(("dom", "grp"), None),
            P(("dom", "grp")),
            P(None, ("dom", "grp")),
            P(None, ("dom", "grp"), None),
            P(None, ("dom", "grp")),
            P("dom", None),
            P(),
        ),
        out_specs=(
            P(("dom", "grp"), None),
            P(("dom", "grp")),
            P(("dom", "grp"), None),
            P(("dom", "grp")),
        ),
        check_vma=False,
    )
```

```python
import functools

import jax
import jax.numpy as jnp
from jax import lax
from jax.experimental import pallas as pl
from jax.experimental.pallas import tpu as pltpu
from jax.sharding import PartitionSpec as P

LEARN = 0.1
LOW = -1e30
ROWS, STATS, SUMS, BACK, HOME, NAMES, GROUP, PASS, PART, FULL, STATE, BACK_LATE, HOME_LATE, KINDS = range(14)
NT = (((1,), (1,)), ((), ()))


def train_kernel(
    n_dom,
    n_grp,
    rounds,
    plan,
    negs,
    pair_source,
    pair_owner,
    pair_offset,
    src_in,
    src_state_in,
    tgt_in,
    tgt_state_in,
    src,
    src_state,
    tgt,
    tgt_state,
    name_all,
    mult,
    tgt_bf,
    tgt_rows,
    row_all,
    full_all,
    state_all,
    src_all,
    scores,
    exps,
    pulls,
    counts,
    exp_grads,
    pull_grads,
    scaled,
    stat_all,
    sum_all,
    part_own,
    part_got,
    back_out,
    back_all,
    home_all,
    send_sem,
    recv_sem,
):
    my_dom = lax.axis_index("dom")
    my_grp = lax.axis_index("grp")
    chips = n_grp // 2
    my_chip, my_core = my_grp // 2, lax.rem(my_grp, 2)
    sibling = my_chip * 2 + 1 - my_core
    width, src_dev = src.shape
    tgt_dev = tgt.shape[1]
    tile = 256
    tiles = tgt_dev // tile
    both = 2 * src_dev
    src_part = n_grp * src_dev
    f32, bf16 = jnp.float32, jnp.bfloat16

    def peers(axis, body):
        size, me = (n_dom, my_dom) if axis == "dom" else (n_grp, my_grp)

        @pl.loop(1, size)
        def _(step):
            body(step, lax.rem(me + step, size))

    def copy(kind, r, axis, step, peer, source, target):
        return pltpu.make_async_remote_copy(
            src_ref=source,
            dst_ref=target,
            send_sem=send_sem.at[r, kind, step],
            recv_sem=recv_sem.at[r, kind, step],
            device_id={axis: peer},
            device_id_type=pl.DeviceIdType.MESH,
        )

    def spread(kind, r, axis, ref):
        peers(axis, lambda step, peer: copy(kind, r, axis, step, peer, ref, ref).start())

    def gathered(kind, r, axis, ref):
        peers(axis, lambda step, peer: copy(kind, r, axis, step, peer, ref, ref).wait())

    def span(index, size):
        return pl.ds(pl.multiple_of(index * size, size), size)

    def rows_of(index):
        return span(index, tile)

    def count_pairs(r, first, last):
        @pl.loop(first, last)
        def _(g):
            source = name_all[g, 0, pl.ds(r, 1), :]
            target = name_all[g, 1, pl.ds(r, 1), :] - my_grp * tgt_dev
            pairs = source.shape[1]
            source_hot = jnp.where(
                lax.broadcasted_iota(jnp.int32, (src_dev, pairs), 0) == source, 1.0, 0.0
            ).astype(bf16)

            @pl.loop(0, tiles)
            def _(i):
                target_hot = jnp.where(
                    lax.broadcasted_iota(jnp.int32, (tile, pairs), 0) == target - i * tile, 1.0, 0.0
                ).astype(bf16)
                counts[rows_of(i), span(g, src_dev)] = lax.dot_general(
                    target_hot, source_hot, NT, preferred_element_type=f32
                ).astype(bf16)

    barrier = pltpu.get_barrier_semaphore()

    def greet(axis):
        def body(step, peer):
            pl.semaphore_signal(
                barrier, inc=1, device_id={axis: peer}, device_id_type=pl.DeviceIdType.MESH
            )

        peers(axis, body)

    greet("dom")
    greet("grp")
    row_all[my_dom] = src_in[...].astype(bf16)
    full_all[my_dom] = src_in[...]
    state_all[my_dom] = src_state_in[...]
    name_all[my_grp, 0] = pair_source[...]
    for r in range(rounds):
        name_all[my_grp, 1, r : r + 1] = pair_owner[r] * tgt_dev + pair_offset[r : r + 1]
    pl.semaphore_wait(barrier, n_dom + n_grp - 2)
    spread(ROWS, 0, "dom", row_all.at[my_dom])
    spread(NAMES, 0, "grp", name_all.at[my_grp])

    @pl.loop(0, tiles)
    def _(i):
        here = lax.broadcasted_iota(jnp.int32, (tile, negs.shape[1]), 0)
        wanted = negs[...] - (my_grp * tgt_dev + i * tile)
        mult[rows_of(i)] = jnp.sum(jnp.where(here == wanted, 1.0, 0.0), axis=1, keepdims=True)
        rows = tgt_in[:, rows_of(i)]
        tgt[:, rows_of(i)] = rows
        tgt_bf[:, rows_of(i)] = rows.astype(bf16)
        tgt_rows[rows_of(i)] = rows.T.astype(bf16)

    tgt_state[...] = tgt_state_in[...]
    gathered(NAMES, 0, "grp", name_all.at[my_grp])
    count_pairs(0, 0, chips)
    gathered(ROWS, 0, "dom", row_all.at[my_dom])
    src_all[0, :, span(my_grp, src_dev)] = row_all[plan[0, my_dom]]

    @pl.loop(0, rounds)
    def _(r):
        def column(index):
            return src_all.at[r, :, span(index, src_dev)]

        def to_chip(step):
            peer = lax.rem(my_chip + step, chips) * 2 + my_core
            return copy(GROUP, r, "grp", step, peer, column(my_grp), column(my_grp))

        def to_sibling(step):
            held = lax.rem(my_chip - step + chips, chips) * 2 + my_core
            return copy(PASS, r, "grp", step, sibling, column(held), column(held))

        for step in range(1, chips):
            to_chip(step).start()
        to_sibling(0).start()

        @pl.when(r == 0)
        def _():
            spread(FULL, 0, "dom", full_all.at[my_dom])
            spread(STATE, 0, "dom", state_all.at[my_dom])

            count_pairs(0, chips, n_grp)

        def score_chip(chip):
            columns = span(chip, both)

            def score(i, top):
                found = jnp.dot(
                    tgt_rows[rows_of(i)], src_all[r, :, columns], preferred_element_type=f32
                )
                scores[rows_of(i), columns] = found
                named = jnp.where(mult[rows_of(i)] > 0, found, LOW)
                return jnp.maximum(top, jnp.max(named, axis=0, keepdims=True))

            top = lax.fori_loop(0, tiles, score, jnp.full((1, both), LOW, f32))

            def add_exp(i, total):
                many = mult[rows_of(i)]
                named = jnp.where(many > 0, scores[rows_of(i), columns], LOW)
                grown = many * jnp.exp(named - top)
                exps[rows_of(i), columns] = grown.astype(bf16)
                return total + jnp.sum(grown, axis=0, keepdims=True)

            total = lax.fori_loop(0, tiles, add_exp, jnp.zeros((1, both), f32))
            stat_all[r, my_grp, 0:1, columns] = top
            stat_all[r, my_grp, 1:2, columns] = total

        for step in range(1, chips + 1):
            if step < chips:
                to_chip(step).wait()
                to_sibling(step).start()
            to_sibling(step - 1).wait()
            score_chip(lax.rem(my_chip - (step - 1) + chips, chips))

        spread(STATS, r, "grp", stat_all.at[r, my_grp])

        @pl.loop(0, chips)
        def _(chip):
            columns = span(chip, both)
            exp_grads[:, columns] = jnp.dot(
                tgt_bf[...], exps[:, columns], preferred_element_type=f32
            )

        gathered(STATS, r, "grp", stat_all.at[r, my_grp])
        top = stat_all[r, 0, 0:1, :]
        for g in range(1, n_grp):
            top = jnp.maximum(top, stat_all[r, g, 0:1, :])
        total = jnp.zeros((1, src_part), f32)
        for g in range(n_grp):
            total += stat_all[r, g, 1:2, :] * jnp.exp(stat_all[r, g, 0:1, :] - top)
        log_total = jnp.log(total)
        part = jnp.exp(stat_all[r, my_grp, 0:1, :] - top) / total

        def pull(i, pulled):
            gap = (scores[rows_of(i)] - top) - log_total
            miss = pl.reciprocal(1.0 + jnp.exp(jnp.minimum(gap, 80.0)), approx=True)
            miss = miss * counts[rows_of(i)].astype(f32)
            pulls[rows_of(i)] = miss.astype(bf16)
            return pulled + jnp.sum(miss, axis=0, keepdims=True)

        pulled = lax.fori_loop(0, tiles, pull, jnp.zeros((1, src_part), f32))
        sum_all[r, my_grp] = pulled
        spread(SUMS, r, "grp", sum_all.at[r, my_grp])

        @pl.loop(0, chips)
        def _(chip):
            columns = span(chip, both)
            pull_grads[:, columns] = jnp.dot(
                tgt_bf[...], pulls[:, columns], preferred_element_type=f32
            )

        gathered(SUMS, r, "grp", sum_all.at[r, my_grp])
        pulled = sum_all[r, 0]
        for g in range(1, n_grp):
            pulled += sum_all[r, g]
        sum_all[r, my_grp] = pulled * part
        factor = sum_all.at[r, my_grp]

        mine, other = span(my_core, src_dev), span(1 - my_core, src_dev)

        def give_part(step):
            return copy(
                PART, r, "grp", step, sibling, part_own.at[r, step, :, other], part_got.at[r, step]
            )

        cut = width // 32 * 16
        halves = ((BACK, HOME, pl.ds(0, cut)), (BACK_LATE, HOME_LATE, pl.ds(cut, width - cut)))

        def give_back(step, half):
            peer = lax.rem(my_chip + step, chips) * 2 + my_core
            kind, _, rows = halves[half]
            return copy(
                kind, r, "grp", step, peer, back_out.at[r, step, rows], back_all.at[r, step, rows]
            )

        def chip_sum(step):
            give_part(step).wait()
            return part_own[r, step, :, mine].astype(f32) + part_got[r, step].astype(f32)

        for turn in range(1, chips + 1):
            step = turn % chips
            columns = span(lax.rem(my_chip + step, chips), both)
            part_own[r, step] = (
                exp_grads[:, columns] * factor[:, columns] - pull_grads[:, columns]
            ).astype(bf16)
            give_part(step).start()
            if turn > 1:
                back_out[r, turn - 1] = chip_sum(turn - 1).astype(bf16)
                give_back(turn - 1, 0).start()

        for step in range(1, chips):
            give_back(step, 1).start()

        @pl.when(r + 1 < rounds)
        def _():
            count_pairs(r + 1, 0, chips)

        give_part(0).wait()
        for half in range(2):
            _, kind, rows = halves[half]
            grads = part_own[r, 0, rows, mine].astype(f32) + part_got[r, 0, rows].astype(f32)
            for step in range(1, chips):
                give_back(step, half).wait()
                grads += back_all[r, step, rows].astype(f32)
            home_all[r, my_dom, rows] = grads.astype(bf16)
            spread(kind, r, "dom", home_all.at[r, my_dom, rows])

        scaled[...] = (src_all[r].astype(f32) * factor[...]).astype(bf16)

        @pl.loop(0, tiles)
        def _(i):
            grads = lax.dot_general(
                scaled[...], exps[rows_of(i)], NT, preferred_element_type=f32
            ) - lax.dot_general(src_all[r], pulls[rows_of(i)], NT, preferred_element_type=f32)
            state = tgt_state[:, rows_of(i)] + jnp.sum(grads * grads, axis=0, keepdims=True) / width
            tgt_state[:, rows_of(i)] = state
            rows = tgt[:, rows_of(i)] - grads * (LEARN / jnp.sqrt(state))
            tgt[:, rows_of(i)] = rows

            @pl.when(r + 1 < rounds)
            def _():
                tgt_bf[:, rows_of(i)] = rows.astype(bf16)
                tgt_rows[rows_of(i)] = rows.T.astype(bf16)

        @pl.when(r + 1 < rounds)
        def _():
            count_pairs(r + 1, chips, n_grp)

        @pl.when(r == 0)
        def _():
            gathered(FULL, 0, "dom", full_all.at[my_dom])
            gathered(STATE, 0, "dom", state_all.at[my_dom])

        for _, kind, rows in halves:
            gathered(kind, r, "dom", home_all.at[r, my_dom, rows])

        @pl.loop(0, n_dom)
        def _(p):
            grads = home_all[r, 0].astype(f32)
            for d in range(1, n_dom):
                grads = jnp.where(plan[r, d] == p, home_all[r, d].astype(f32), grads)
            state = state_all[p] + jnp.sum(grads * grads, axis=0, keepdims=True) / width
            state_all[p] = state
            full_all[p] = full_all[p] - grads * (LEARN / jnp.sqrt(state))

        @pl.when(r + 1 < rounds)
        def _():
            src_all[r + 1, :, span(my_grp, src_dev)] = full_all[plan[r + 1, my_dom]].astype(bf16)

    src[...] = full_all[my_dom]
    src_state[...] = state_all[my_dom]


def hand_out(*refs):
    for source, target in zip(refs[:4], refs[4:]):
        target[...] = source[...]


def shards(
    n_dom,
    n_grp,
    src_table,
    src_state,
    tgt_table,
    tgt_state,
    pair_source,
    pair_owner,
    pair_offset,
    negatives,
    plan,
):
    rounds, pairs = pair_source.shape
    src_dev, width = src_table.shape
    tgt_dev = tgt_table.shape[0]
    src_part = n_grp * src_dev
    chips = n_grp // 2
    f32, bf16 = jnp.float32, jnp.bfloat16
    vmem = pl.BlockSpec(memory_space=pltpu.VMEM)
    steps = max(n_dom, n_grp)
    trained = pl.pallas_call(
        functools.partial(train_kernel, n_dom, n_grp, rounds),
        out_shape=(
            jax.ShapeDtypeStruct((width, src_dev), f32),
            jax.ShapeDtypeStruct((1, src_dev), f32),
            jax.ShapeDtypeStruct((width, tgt_dev), f32),
            jax.ShapeDtypeStruct((1, tgt_dev), f32),
        ),
        in_specs=[pl.BlockSpec(memory_space=pltpu.SMEM)] + [vmem] * 8,
        out_specs=[vmem] * 4,
        scratch_shapes=[
            pltpu.VMEM((n_grp, 2, rounds, pairs), jnp.int32),
            pltpu.VMEM((tgt_dev, 1), f32),
            pltpu.VMEM((width, tgt_dev), bf16),
            pltpu.VMEM((tgt_dev, width), bf16),
            pltpu.VMEM((n_dom, width, src_dev), bf16),
            pltpu.VMEM((n_dom, width, src_dev), f32),
            pltpu.VMEM((n_dom, 1, src_dev), f32),
            pltpu.VMEM((rounds, width, src_part), bf16),
            pltpu.VMEM((tgt_dev, src_part), f32),
            pltpu.VMEM((tgt_dev, src_part), bf16),
            pltpu.VMEM((tgt_dev, src_part), bf16),
            pltpu.VMEM((tgt_dev, src_part), bf16),
            pltpu.VMEM((width, src_part), f32),
            pltpu.VMEM((width, src_part), f32),
            pltpu.VMEM((width, src_part), bf16),
            pltpu.VMEM((rounds, n_grp, 2, src_part), f32),
            pltpu.VMEM((rounds, n_grp, 1, src_part), f32),
            pltpu.VMEM((rounds, chips, width, 2 * src_dev), bf16),
            pltpu.VMEM((rounds, chips, width, src_dev), bf16),
            pltpu.VMEM((rounds, chips, width, src_dev), bf16),
            pltpu.VMEM((rounds, chips, width, src_dev), bf16),
            pltpu.VMEM((rounds, n_dom, width, src_dev), bf16),
            pltpu.SemaphoreType.DMA((rounds, KINDS, steps)),
            pltpu.SemaphoreType.DMA((rounds, KINDS, steps)),
        ],
        compiler_params=pltpu.CompilerParams(
            collective_id=0, has_side_effects=True, vmem_limit_bytes=56 * 1024 * 1024
        ),
        name="train",
    )(
        plan,
        negatives,
        pair_source,
        pair_owner.transpose(0, 2, 1),
        pair_offset,
        src_table.T,
        src_state[None, :],
        tgt_table.T,
        tgt_state[None, :],
    )
    new_src, new_src_state, new_tgt, new_tgt_state = pl.pallas_call(
        hand_out,
        out_shape=[jax.ShapeDtypeStruct(x.shape, x.dtype) for x in trained],
        in_specs=[vmem] * 4,
        out_specs=[vmem] * 4,
        name="hand_out",
    )(*trained)
    return (new_src.T, new_src_state[0], new_tgt.T, new_tgt_state[0])


def solution(mesh):
    return jax.shard_map(
        functools.partial(shards, mesh.shape["dom"], mesh.shape["grp"]),
        mesh=mesh,
        in_specs=(
            P(("dom", "grp"), None),
            P(("dom", "grp")),
            P(("dom", "grp"), None),
            P(("dom", "grp")),
            P(None, ("dom", "grp")),
            P(None, ("dom", "grp"), None),
            P(None, ("dom", "grp")),
            P("dom", None),
            P(),
        ),
        out_specs=(
            P(("dom", "grp"), None),
            P(("dom", "grp")),
            P(("dom", "grp"), None),
            P(("dom", "grp")),
        ),
        check_vma=False,
    )
```

```python
import functools

import jax
import jax.numpy as jnp
from jax import lax
from jax.experimental import pallas as pl
from jax.experimental.pallas import tpu as pltpu
from jax.sharding import PartitionSpec as P

LEARN = 0.1
LOW = -1e30
ROWS, STATS, SUMS, BACK, HOME, NAMES, GROUP, PASS, PART, FULL, STATE, BACK_LATE, HOME_LATE, KINDS = range(14)
NT = (((1,), (1,)), ((), ()))


def train_kernel(
    n_dom,
    n_grp,
    rounds,
    plan,
    negs,
    pair_source,
    pair_owner,
    pair_offset,
    src_in,
    src_state_in,
    tgt_in,
    tgt_state_in,
    src,
    src_state,
    tgt,
    tgt_state,
    name_all,
    mult,
    tgt_bf,
    tgt_rows,
    row_all,
    full_all,
    state_all,
    src_all,
    scores,
    exps,
    pulls,
    counts,
    exp_grads,
    pull_grads,
    scaled,
    stat_all,
    sum_all,
    part_own,
    part_got,
    back_out,
    back_all,
    home_all,
    send_sem,
    recv_sem,
):
    my_dom = lax.axis_index("dom")
    my_grp = lax.axis_index("grp")
    chips = n_grp // 2
    my_chip, my_core = my_grp // 2, lax.rem(my_grp, 2)
    sibling = my_chip * 2 + 1 - my_core
    width, src_dev = src.shape
    tgt_dev = tgt.shape[1]
    tile = 256
    tiles = tgt_dev // tile
    both = 2 * src_dev
    src_part = n_grp * src_dev
    f32, bf16 = jnp.float32, jnp.bfloat16

    def peers(axis, body):
        size, me = (n_dom, my_dom) if axis == "dom" else (n_grp, my_grp)

        @pl.loop(1, size)
        def _(step):
            body(step, lax.rem(me + step, size))

    def copy(kind, r, axis, step, peer, source, target):
        return pltpu.make_async_remote_copy(
            src_ref=source,
            dst_ref=target,
            send_sem=send_sem.at[r, kind, step],
            recv_sem=recv_sem.at[r, kind, step],
            device_id={axis: peer},
            device_id_type=pl.DeviceIdType.MESH,
        )

    def spread(kind, r, axis, ref):
        peers(axis, lambda step, peer: copy(kind, r, axis, step, peer, ref, ref).start())

    def gathered(kind, r, axis, ref):
        peers(axis, lambda step, peer: copy(kind, r, axis, step, peer, ref, ref).wait())

    def span(index, size):
        return pl.ds(pl.multiple_of(index * size, size), size)

    def rows_of(index):
        return span(index, tile)

    def count_pairs(r, first, last):
        @pl.loop(first, last)
        def _(g):
            source = name_all[g, 0, pl.ds(r, 1), :]
            target = name_all[g, 1, pl.ds(r, 1), :] - my_grp * tgt_dev
            pairs = source.shape[1]
            source_hot = jnp.where(
                lax.broadcasted_iota(jnp.int32, (src_dev, pairs), 0) == source, 1.0, 0.0
            ).astype(bf16)

            @pl.loop(0, tiles, unroll=True)
            def _(i):
                target_hot = jnp.where(
                    lax.broadcasted_iota(jnp.int32, (tile, pairs), 0) == target - i * tile, 1.0, 0.0
                ).astype(bf16)
                counts[rows_of(i), span(g, src_dev)] = lax.dot_general(
                    target_hot, source_hot, NT, preferred_element_type=f32
                ).astype(bf16)

    barrier = pltpu.get_barrier_semaphore()

    def greet(axis):
        def body(step, peer):
            pl.semaphore_signal(
                barrier, inc=1, device_id={axis: peer}, device_id_type=pl.DeviceIdType.MESH
            )

        peers(axis, body)

    greet("dom")
    greet("grp")
    row_all[my_dom] = src_in[...].astype(bf16)
    full_all[my_dom] = src_in[...]
    state_all[my_dom] = src_state_in[...]
    name_all[my_grp, 0] = pair_source[...]
    for r in range(rounds):
        name_all[my_grp, 1, r : r + 1] = pair_owner[r] * tgt_dev + pair_offset[r : r + 1]
    pl.semaphore_wait(barrier, n_dom + n_grp - 2)
    spread(ROWS, 0, "dom", row_all.at[my_dom])
    spread(NAMES, 0, "grp", name_all.at[my_grp])

    @pl.loop(0, tiles, unroll=True)
    def _(i):
        here = lax.broadcasted_iota(jnp.int32, (tile, negs.shape[1]), 0)
        wanted = negs[...] - (my_grp * tgt_dev + i * tile)
        mult[rows_of(i)] = jnp.sum(jnp.where(here == wanted, 1.0, 0.0), axis=1, keepdims=True)
        rows = tgt_in[:, rows_of(i)]
        tgt[:, rows_of(i)] = rows
        tgt_bf[:, rows_of(i)] = rows.astype(bf16)
        tgt_rows[rows_of(i)] = rows.T.astype(bf16)

    tgt_state[...] = tgt_state_in[...]
    gathered(NAMES, 0, "grp", name_all.at[my_grp])
    count_pairs(0, 0, chips)
    gathered(ROWS, 0, "dom", row_all.at[my_dom])
    src_all[0, :, span(my_grp, src_dev)] = row_all[plan[0, my_dom]]

    @pl.loop(0, rounds)
    def _(r):
        def column(index):
            return src_all.at[r, :, span(index, src_dev)]

        def to_chip(step):
            peer = lax.rem(my_chip + step, chips) * 2 + my_core
            return copy(GROUP, r, "grp", step, peer, column(my_grp), column(my_grp))

        def to_sibling(step):
            held = lax.rem(my_chip - step + chips, chips) * 2 + my_core
            return copy(PASS, r, "grp", step, sibling, column(held), column(held))

        for step in range(1, chips):
            to_chip(step).start()
        to_sibling(0).start()

        @pl.when(r == 0)
        def _():
            spread(FULL, 0, "dom", full_all.at[my_dom])
            spread(STATE, 0, "dom", state_all.at[my_dom])

            count_pairs(0, chips, n_grp)

        def score_chip(chip):
            columns = span(chip, both)

            def score(i, top):
                found = jnp.dot(
                    tgt_rows[rows_of(i)], src_all[r, :, columns], preferred_element_type=f32
                )
                scores[rows_of(i), columns] = found
                named = jnp.where(mult[rows_of(i)] > 0, found, LOW)
                return jnp.maximum(top, jnp.max(named, axis=0, keepdims=True))

            top = lax.fori_loop(0, tiles, score, jnp.full((1, both), LOW, f32), unroll=True)

            def add_exp(i, total):
                many = mult[rows_of(i)]
                named = jnp.where(many > 0, scores[rows_of(i), columns], LOW)
                grown = many * jnp.exp(named - top)
                exps[rows_of(i), columns] = grown.astype(bf16)
                return total + jnp.sum(grown, axis=0, keepdims=True)

            total = lax.fori_loop(0, tiles, add_exp, jnp.zeros((1, both), f32), unroll=True)
            stat_all[r, my_grp, 0:1, columns] = top
            stat_all[r, my_grp, 1:2, columns] = total

        for step in range(1, chips + 1):
            if step < chips:
                to_chip(step).wait()
                to_sibling(step).start()
            to_sibling(step - 1).wait()
            score_chip(lax.rem(my_chip - (step - 1) + chips, chips))

        spread(STATS, r, "grp", stat_all.at[r, my_grp])

        @pl.loop(0, chips, unroll=True)
        def _(chip):
            columns = span(chip, both)
            exp_grads[:, columns] = jnp.dot(
                tgt_bf[...], exps[:, columns], preferred_element_type=f32
            )

        gathered(STATS, r, "grp", stat_all.at[r, my_grp])
        top = stat_all[r, 0, 0:1, :]
        for g in range(1, n_grp):
            top = jnp.maximum(top, stat_all[r, g, 0:1, :])
        total = jnp.zeros((1, src_part), f32)
        for g in range(n_grp):
            total += stat_all[r, g, 1:2, :] * jnp.exp(stat_all[r, g, 0:1, :] - top)
        log_total = jnp.log(total)
        part = jnp.exp(stat_all[r, my_grp, 0:1, :] - top) / total

        def pull(i, pulled):
            gap = (scores[rows_of(i)] - top) - log_total
            miss = pl.reciprocal(1.0 + jnp.exp(jnp.minimum(gap, 80.0)), approx=True)
            miss = miss * counts[rows_of(i)].astype(f32)
            pulls[rows_of(i)] = miss.astype(bf16)
            return pulled + jnp.sum(miss, axis=0, keepdims=True)

        pulled = lax.fori_loop(0, tiles, pull, jnp.zeros((1, src_part), f32), unroll=True)
        sum_all[r, my_grp] = pulled
        spread(SUMS, r, "grp", sum_all.at[r, my_grp])

        @pl.loop(0, chips, unroll=True)
        def _(chip):
            columns = span(chip, both)
            pull_grads[:, columns] = jnp.dot(
                tgt_bf[...], pulls[:, columns], preferred_element_type=f32
            )

        gathered(SUMS, r, "grp", sum_all.at[r, my_grp])
        pulled = sum_all[r, 0]
        for g in range(1, n_grp):
            pulled += sum_all[r, g]
        sum_all[r, my_grp] = pulled * part
        factor = sum_all.at[r, my_grp]

        mine, other = span(my_core, src_dev), span(1 - my_core, src_dev)

        def give_part(step):
            return copy(
                PART, r, "grp", step, sibling, part_own.at[r, step, :, other], part_got.at[r, step]
            )

        cut = width // 32 * 16
        halves = ((BACK, HOME, pl.ds(0, cut)), (BACK_LATE, HOME_LATE, pl.ds(cut, width - cut)))

        def give_back(step, half):
            peer = lax.rem(my_chip + step, chips) * 2 + my_core
            kind, _, rows = halves[half]
            return copy(
                kind, r, "grp", step, peer, back_out.at[r, step, rows], back_all.at[r, step, rows]
            )

        def chip_sum(step):
            give_part(step).wait()
            return part_own[r, step, :, mine].astype(f32) + part_got[r, step].astype(f32)

        for turn in range(1, chips + 1):
            step = turn % chips
            columns = span(lax.rem(my_chip + step, chips), both)
            part_own[r, step] = (
                exp_grads[:, columns] * factor[:, columns] - pull_grads[:, columns]
            ).astype(bf16)
            give_part(step).start()
            if turn > 1:
                back_out[r, turn - 1] = chip_sum(turn - 1).astype(bf16)
                give_back(turn - 1, 0).start()

        for step in range(1, chips):
            give_back(step, 1).start()

        @pl.when(r + 1 < rounds)
        def _():
            count_pairs(r + 1, 0, chips)

        give_part(0).wait()
        for half in range(2):
            _, kind, rows = halves[half]
            grads = part_own[r, 0, rows, mine].astype(f32) + part_got[r, 0, rows].astype(f32)
            for step in range(1, chips):
                give_back(step, half).wait()
                grads += back_all[r, step, rows].astype(f32)
            home_all[r, my_dom, rows] = grads.astype(bf16)
            spread(kind, r, "dom", home_all.at[r, my_dom, rows])

        scaled[...] = (src_all[r].astype(f32) * factor[...]).astype(bf16)

        @pl.loop(0, tiles, unroll=True)
        def _(i):
            grads = lax.dot_general(
                scaled[...], exps[rows_of(i)], NT, preferred_element_type=f32
            ) - lax.dot_general(src_all[r], pulls[rows_of(i)], NT, preferred_element_type=f32)
            state = tgt_state[:, rows_of(i)] + jnp.sum(grads * grads, axis=0, keepdims=True) / width
            tgt_state[:, rows_of(i)] = state
            rows = tgt[:, rows_of(i)] - grads * (LEARN / jnp.sqrt(state))
            tgt[:, rows_of(i)] = rows

            @pl.when(r + 1 < rounds)
            def _():
                tgt_bf[:, rows_of(i)] = rows.astype(bf16)
                tgt_rows[rows_of(i)] = rows.T.astype(bf16)

        @pl.when(r + 1 < rounds)
        def _():
            count_pairs(r + 1, chips, n_grp)

        @pl.when(r == 0)
        def _():
            gathered(FULL, 0, "dom", full_all.at[my_dom])
            gathered(STATE, 0, "dom", state_all.at[my_dom])

        for _, kind, rows in halves:
            gathered(kind, r, "dom", home_all.at[r, my_dom, rows])

        @pl.loop(0, n_dom)
        def _(p):
            grads = home_all[r, 0].astype(f32)
            for d in range(1, n_dom):
                grads = jnp.where(plan[r, d] == p, home_all[r, d].astype(f32), grads)
            state = state_all[p] + jnp.sum(grads * grads, axis=0, keepdims=True) / width
            state_all[p] = state
            full_all[p] = full_all[p] - grads * (LEARN / jnp.sqrt(state))

        @pl.when(r + 1 < rounds)
        def _():
            src_all[r + 1, :, span(my_grp, src_dev)] = full_all[plan[r + 1, my_dom]].astype(bf16)

    src[...] = full_all[my_dom]
    src_state[...] = state_all[my_dom]


def hand_out(*refs):
    for source, target in zip(refs[:4], refs[4:]):
        target[...] = source[...]


def shards(
    n_dom,
    n_grp,
    src_table,
    src_state,
    tgt_table,
    tgt_state,
    pair_source,
    pair_owner,
    pair_offset,
    negatives,
    plan,
):
    rounds, pairs = pair_source.shape
    src_dev, width = src_table.shape
    tgt_dev = tgt_table.shape[0]
    src_part = n_grp * src_dev
    chips = n_grp // 2
    f32, bf16 = jnp.float32, jnp.bfloat16
    vmem = pl.BlockSpec(memory_space=pltpu.VMEM)
    steps = max(n_dom, n_grp)
    trained = pl.pallas_call(
        functools.partial(train_kernel, n_dom, n_grp, rounds),
        out_shape=(
            jax.ShapeDtypeStruct((width, src_dev), f32),
            jax.ShapeDtypeStruct((1, src_dev), f32),
            jax.ShapeDtypeStruct((width, tgt_dev), f32),
            jax.ShapeDtypeStruct((1, tgt_dev), f32),
        ),
        in_specs=[pl.BlockSpec(memory_space=pltpu.SMEM)] + [vmem] * 8,
        out_specs=[vmem] * 4,
        scratch_shapes=[
            pltpu.VMEM((n_grp, 2, rounds, pairs), jnp.int32),
            pltpu.VMEM((tgt_dev, 1), f32),
            pltpu.VMEM((width, tgt_dev), bf16),
            pltpu.VMEM((tgt_dev, width), bf16),
            pltpu.VMEM((n_dom, width, src_dev), bf16),
            pltpu.VMEM((n_dom, width, src_dev), f32),
            pltpu.VMEM((n_dom, 1, src_dev), f32),
            pltpu.VMEM((rounds, width, src_part), bf16),
            pltpu.VMEM((tgt_dev, src_part), f32),
            pltpu.VMEM((tgt_dev, src_part), bf16),
            pltpu.VMEM((tgt_dev, src_part), bf16),
            pltpu.VMEM((tgt_dev, src_part), bf16),
            pltpu.VMEM((width, src_part), f32),
            pltpu.VMEM((width, src_part), f32),
            pltpu.VMEM((width, src_part), bf16),
            pltpu.VMEM((rounds, n_grp, 2, src_part), f32),
            pltpu.VMEM((rounds, n_grp, 1, src_part), f32),
            pltpu.VMEM((rounds, chips, width, 2 * src_dev), bf16),
            pltpu.VMEM((rounds, chips, width, src_dev), bf16),
            pltpu.VMEM((rounds, chips, width, src_dev), bf16),
            pltpu.VMEM((rounds, chips, width, src_dev), bf16),
            pltpu.VMEM((rounds, n_dom, width, src_dev), bf16),
            pltpu.SemaphoreType.DMA((rounds, KINDS, steps)),
            pltpu.SemaphoreType.DMA((rounds, KINDS, steps)),
        ],
        compiler_params=pltpu.CompilerParams(
            collective_id=0, has_side_effects=True, vmem_limit_bytes=56 * 1024 * 1024
        ),
        name="train",
    )(
        plan,
        negatives,
        pair_source,
        pair_owner.transpose(0, 2, 1),
        pair_offset,
        src_table.T,
        src_state[None, :],
        tgt_table.T,
        tgt_state[None, :],
    )
    new_src, new_src_state, new_tgt, new_tgt_state = pl.pallas_call(
        hand_out,
        out_shape=[jax.ShapeDtypeStruct(x.shape, x.dtype) for x in trained],
        in_specs=[vmem] * 4,
        out_specs=[vmem] * 4,
        name="hand_out",
    )(*trained)
    return (new_src.T, new_src_state[0], new_tgt.T, new_tgt_state[0])


def solution(mesh):
    return jax.shard_map(
        functools.partial(shards, mesh.shape["dom"], mesh.shape["grp"]),
        mesh=mesh,
        in_specs=(
            P(("dom", "grp"), None),
            P(("dom", "grp")),
            P(("dom", "grp"), None),
            P(("dom", "grp")),
            P(None, ("dom", "grp")),
            P(None, ("dom", "grp"), None),
            P(None, ("dom", "grp")),
            P("dom", None),
            P(),
        ),
        out_specs=(
            P(("dom", "grp"), None),
            P(("dom", "grp")),
            P(("dom", "grp"), None),
            P(("dom", "grp")),
        ),
        check_vma=False,
    )
```
